32 devices in a mesh: cuts: 2 (over y), leg: 8 (over z, x), sub: 2 (over core).
Axes of the slice: x: 2, y: 2, z: 4, core: 2. Of those that a mesh axis runs over, the one named last changes fastest.
Arguments:
- stem_tensor: bfloat16 [2, 32768, 512], P(None, ('cuts', 'leg', 'sub')), parts along dimension 1, may hold values from -6 to 6
- branches: bfloat16 [3, 2, 2, 512, 512], P(None, None, None, 'leg', 'sub'), may hold values from -0.1875 to 0.1875
- contraction_order: int32 [3], replicated, may hold values from 0 to 2, each once
- cut_values: int32 [6], P('cuts'), parts along dimension 0, may hold values from 0 to 1
Outputs:
- contracted: bfloat16 [2, 32768, 512], P(None, ('cuts', 'leg', 'sub')), parts along dimension 1
The draws below stay inside these ranges and needn't reach their ends.
There are 2 independent parts, one for each index of `cuts`. The reference program is written for one: setup_inputs(seed, part) draws one part's arguments, and reference() takes and returns one part's arrays. A program takes and returns all parts, laid end to end along the dimension named above; an argument that names none is the same for every part. Nothing has to cross between parts.
Inputs may be any that keep to these rules, and one draw needn't show every extreme that they name: `contraction_order`: a permutation of 0 to 2.
All inputs are finite; a program needn't handle non-finite values.
Results may differ from the reference program's by a relative error of at most 0.0058.
Values may be sent and summed in bfloat16 or wider, within the bound.
A program may use at most 64 MiB of HBM per device.

```python
import jax
import jax.numpy as jnp

STEPS = 3
COLS = 512
STEM_ROWS = 16384
N_LEG = 8
N_SUB = 2


def shard_levels(key, dims, cuts, least, largest):
    loudness = 1.0
    for position, parts in cuts:
        heights = jax.random.uniform(jax.random.fold_in(jax.random.fold_in(key, 6), position), (parts,), jnp.float32, least / len(cuts), largest / len(cuts))
        loudness = loudness * jnp.repeat(jnp.exp(heights), dims[position] // parts).reshape((-1,) + (1,) * (len(dims) - 1 - position))
    return loudness


def normal_values(rng, shape, spread, bound, cuts=(), kind=jnp.bfloat16):
    result = spread * jax.random.normal(rng, shape, jnp.float32)
    if cuts:
        result = result * shard_levels(rng, shape, cuts, -0.22, 0.18)
    return jnp.clip(result, -bound, bound).astype(kind)


def setup_inputs(seed: int = 0, part: int = 0) -> dict:
    splits = jax.random.split(jax.random.key(seed), 5)
    part_splits = jax.random.split(jax.random.fold_in(splits[4], part), 5)
    stem_tensor = normal_values(part_splits[0], (2, STEM_ROWS, COLS), 1.0, 6.0, ((1, 16),))
    branches = normal_values(splits[1], (STEPS, 2, 2, COLS, COLS), (2 * COLS) ** -0.5, 0.1875, ((3, 8), (4, 2)))
    contraction_order = jax.random.permutation(splits[2], STEPS).astype(jnp.int32)
    cut_values = jax.random.randint(part_splits[3], (STEPS,), 0, 2).astype(jnp.int32)
    return {"stem_tensor": stem_tensor, "branches": branches, "contraction_order": contraction_order, "cut_values": cut_values}


def permute_legs(flat, high_bits, low_size, rotation):
    lead = flat.shape[:-1]
    lead_count = len(lead)
    split = flat.reshape(lead + (2,) * high_bits + (low_size,))
    axes = list(range(lead_count))
    for dest_pos in range(high_bits):
        dest_bit = high_bits - 1 - dest_pos
        source_bit = (dest_bit + rotation) % high_bits
        axes.append(lead_count + high_bits - 1 - source_bit)
    axes.append(lead_count + high_bits)
    return jnp.transpose(split, axes).reshape(flat.shape)


def complex_matrix(complex_block):
    real_part = complex_block[0]
    imag_part = complex_block[1]
    upper = jnp.concatenate([real_part, imag_part], 1)
    lower = jnp.concatenate([-imag_part, real_part], 1)
    return jnp.concatenate([upper, lower], 0)


def reference(stem_tensor, branches, contraction_order, cut_values):
    dev_count = N_LEG * N_SUB
    row_count = stem_tensor.shape[1] // dev_count
    col_count = stem_tensor.shape[2]
    low_size = col_count // 4
    high_bits = (row_count * col_count // low_size).bit_length() - 1
    current = stem_tensor
    for section_index in range(STEPS):
        flattened = current.reshape(2, dev_count, row_count * col_count)
        permuted = permute_legs(flattened, high_bits, low_size, 2 * section_index + 3)
        blocks = permuted.reshape(2, dev_count, dev_count, row_count // dev_count, col_count)
        regrouped = jnp.swapaxes(blocks, 1, 2).reshape(2, dev_count * row_count, col_count)
        matrix = complex_matrix(branches[contraction_order[section_index], cut_values[section_index]])
        operand = jnp.concatenate([regrouped[0], regrouped[1]], 1)
        product = jnp.dot(operand, matrix, preferred_element_type=jnp.float32)
        current = jnp.stack([product[:, :col_count], product[:, col_count:]]).astype(jnp.bfloat16)
    return current
```

```python
import jax
import jax.numpy as jnp
from jax import lax
from jax.experimental import pallas as pl
from jax.experimental.pallas import tpu as pltpu
from jax.sharding import PartitionSpec as P

STEPS = 3
MESH = pl.DeviceIdType.MESH


def permute_legs(flat, high_bits, low_size, rotation):
    lead = flat.shape[:-1]
    lead_count = len(lead)
    split = flat.reshape(lead + (2,) * high_bits + (low_size,))
    axes = list(range(lead_count))
    for dest_pos in range(high_bits):
        dest_bit = high_bits - 1 - dest_pos
        source_bit = (dest_bit + rotation) % high_bits
        axes.append(lead_count + high_bits - 1 - source_bit)
    axes.append(lead_count + high_bits)
    return jnp.transpose(split, axes).reshape(flat.shape)


def complex_matrix(complex_block):
    real_part = complex_block[0]
    imag_part = complex_block[1]
    upper = jnp.concatenate([real_part, imag_part], 1)
    lower = jnp.concatenate([-imag_part, real_part], 1)
    return jnp.concatenate([upper, lower], 0)


def fold_rows(stem_rows, shard_piece):
    operand = jnp.concatenate([stem_rows[0], stem_rows[1]], 1)
    return jnp.dot(operand, complex_matrix(shard_piece), preferred_element_type=jnp.float32)


def shards(stem_tensor, branches, contraction_order, cut_values):
    row_count = stem_tensor.shape[1]
    col_count = stem_tensor.shape[2]
    low_size = col_count // 4
    high_bits = (row_count * col_count // low_size).bit_length() - 1
    leg_count = lax.axis_size("leg")
    core_count = lax.axis_size("sub")
    dev_count = leg_count * core_count
    current = stem_tensor
    for section_index in range(STEPS):
        flattened = current.reshape(2, row_count * col_count)
        permuted = permute_legs(flattened, high_bits, low_size, 2 * section_index + 3)
        blocks = permuted.reshape(2, dev_count, row_count // dev_count, col_count)
        arrived = lax.all_to_all(blocks, ("leg", "sub"), split_axis=1, concat_axis=1, tiled=True)
        regrouped = arrived.reshape(2, row_count, col_count)
        chosen = branches[contraction_order[section_index], cut_values[section_index]]
        branch_part = lax.all_gather(chosen, "sub", axis=2, tiled=True)
        new_width = branch_part.shape[2]
        product = fold_rows(regrouped, lax.all_gather(branch_part, "leg", axis=1, tiled=True))
        current = jnp.stack([product[:, :new_width], product[:, new_width:]]).astype(jnp.bfloat16)
    return current


def follow_legs(block_bits, high_bits):
    block = ["D%d" % i for i in range(block_bits)]
    local = ["H%d" % i for i in range(high_bits)]
    summed = []
    for step in range(STEPS):
        local = [local[(b + 2 * step + 3) % high_bits] for b in range(high_bits)]
        lead = local[high_bits - block_bits :]
        local = local[: high_bits - block_bits] + block
        block = lead
        summed.append(tuple(local[:2]))
        local[:2] = ["ABC"[step] + "0", "ABC"[step] + "1"]
    return summed, block, local


def stays_home(block_count, rows, cols):
    high_bits = (rows * 4).bit_length() - 1
    block_bits = block_count.bit_length() - 1
    if cols != 512 or rows != 1024 or block_bits > high_bits:
        return False
    summed, block, local = follow_legs(block_bits, high_bits)
    return (
        summed == [("H3", "H4"), ("H8", "H9"), ("A0", "H11")]
        and block == ["D%d" % i for i in range(block_bits)]
        and local == ["C0", "C1", "H0", "H1", "H2", "B0", "B1", "H10", "A1", "H5", "H6", "H7"]
    )


CHUNKS = 4
PART = 256


def tile(values, row, col):
    return values[col // 2][row : row + 8, (col % 2) * 128 : (col % 2 + 1) * 128]


def gather_rows(xs, lhs, g):
    for q in range(2):
        for m in range(4):
            pieces = []
            for r in range(32):
                h9, h8, h11, h5, h10 = [(r >> s) & 1 for s in (4, 3, 2, 1, 0)]
                h = (h11 << 11) + (h10 << 10) + (h9 << 9) + (h8 << 8) + (g << 6) + (h5 << 5) + (m << 3)
                pieces.append(xs[q, h : h + 8, :])
            col = q * 4 + m
            lhs[g, :, col * 128 : (col + 1) * 128] = jnp.concatenate(pieces, 0).astype(jnp.bfloat16)


def next_rows_0(values, q, lhs, g):
    for m in range(4):
        pieces = []
        for r in range(32):
            h11, a0, h5, a1, h10 = [(r >> s) & 1 for s in (4, 3, 2, 1, 0)]
            pieces.append(tile(values, m * 64 + (h11 * 4 + h5 * 2 + h10) * 8, a1 * 2 + a0))
        col = q * 4 + m
        lhs[g, :, col * 128 : (col + 1) * 128] = jnp.concatenate(pieces, 0).astype(jnp.bfloat16)


def next_rows_1(values, q, lhs, g):
    for m in range(4):
        pieces = []
        for r in range(32):
            row, b = r >> 2, r & 3
            pieces.append(tile(values, m * 64 + row * 8, b))
        col = q * 4 + m
        lhs[g, :, col * 128 : (col + 1) * 128] = jnp.concatenate(pieces, 0).astype(jnp.bfloat16)


def kernel(order_in, cut_in, stem, shard_in, out, order, cut, shard, x, xs, lhs_a, lhs_b, held, neg, result, in_sem, out_sem, send, recv):
    leg = lax.axis_index("leg")
    sub = lax.axis_index("sub")
    spot = leg // 2 + (leg % 2) * (7 - 2 * (leg // 2))

    def leg_at(place):
        place = lax.rem(place + 16, 8)
        far = place // 4
        return far * (15 - 2 * place) + (1 - far) * 2 * place

    after = dict(leg=leg_at(spot + 1), sub=sub)
    before = dict(leg=leg_at(spot - 1), sub=sub)
    sibling = dict(leg=leg, sub=1 - sub)

    barrier = pltpu.get_barrier_semaphore()
    for peer in (after, before, sibling):
        pl.semaphore_signal(barrier, inc=1, device_id=peer, device_id_type=MESH)

    loads = [
        pltpu.make_async_copy(source, target, in_sem.at[i])
        for i, (source, target) in enumerate(((order_in, order), (cut_in, cut), (shard_in, shard), (stem, x)))
    ]
    for load in loads:
        load.start()
    for load in loads[:3]:
        load.wait()
    for step in range(STEPS):
        chosen = shard[order[step], cut[step]]
        held[step, sub, leg, 0] = chosen[1]
        held[step, sub, leg, 1] = chosen[0]
    pl.semaphore_wait(barrier, 3)

    def copy(ref, step, slot, target):
        return pltpu.make_async_remote_copy(
            src_ref=ref,
            dst_ref=ref,
            send_sem=send.at[step, slot],
            recv_sem=recv.at[step, slot],
            device_id=target,
            device_id_type=MESH,
        )

    def block(step, way, dist, side):
        owner = leg_at(spot - dist if way == 0 else spot + dist)
        if dist == 4:
            return held.at[step, side, owner, way]
        return held.at[step, side, owner]

    def ring(step, way, dist, sending):
        target = after if way == 0 else before
        if sending and dist == 4:
            owner = leg_at(spot - 3 if way == 0 else spot + 3)
            ref = held.at[step, sub, owner, way]
        else:
            ref = block(step, way, dist - 1 if sending else dist, sub)
        return copy(ref, step, way * 4 + dist - 1, target)

    def share(step, way, dist, sending):
        slot = 8 if dist == 0 else 8 + way * 4 + dist
        return copy(block(step, way, dist, sub if sending else 1 - sub), step, slot, sibling)

    def send_own(step):
        for way in range(2):
            ring(step, way, 1, True).start()
        share(step, 0, 0, True).start()

    def take(step, dist):
        for way in range(2):
            ring(step, way, dist, False).wait_recv()
            if dist < 4:
                ring(step, way, dist + 1, True).start()
            share(step, way, dist, True).start()

    def take_shared(step):
        share(step, 0, 0, False).wait_recv()
        for dist in range(1, 5):
            for way in range(2):
                share(step, way, dist, False).wait_recv()

    def finish(step):
        share(step, 0, 0, True).wait_send()
        for dist in range(1, 5):
            for way in range(2):
                ring(step, way, dist, True).wait_send()
                share(step, way, dist, True).wait_send()

    for step in range(STEPS):
        send_own(step)

    loads[3].wait()
    for q in range(2):
        for j in range(4):
            xs[q, pl.ds(j, 1024, 4), :] = x[q, :, j * 128 : (j + 1) * 128].astype(jnp.float32)
    early = [(0, 1), (1, 1), (0, 2), (2, 1), (1, 2), (0, 3), (2, 2), (1, 3)]
    for i, turn in enumerate(early):
        take(*turn)
        if i in (2, 3, 4, 5):
            gather_rows(xs, lhs_a, i - 2)
    between = {(0, 1): (2, 3), (0, 3): (1, 4), (1, 1): (2, 4)}

    now, later = lhs_a, lhs_b
    for step in range(STEPS):
        if step == 0:
            take(0, 4)
        take_shared(step)
        for side in range(2):
            neg[side] = -held[step, side, :, 0]
        for g in range(CHUNKS):
            if (step, g) in between:
                take(*between[step, g])
            lhs = now[g]
            re, im = [], []
            for side in range(2):
                mi = held[step, side, :, 0].reshape(512, 256)
                mr = held[step, side, :, 1].reshape(512, 256)
                w_re = jnp.concatenate([mr, neg[side].reshape(512, 256)], 0)
                w_im = jnp.concatenate([mi, mr], 0)
                re.append(jnp.dot(lhs, w_re, preferred_element_type=jnp.float32))
                im.append(jnp.dot(lhs, w_im, preferred_element_type=jnp.float32))
            if step < STEPS - 1:
                arrange = next_rows_0 if step == 0 else next_rows_1
                arrange(re, 0, later, g)
                arrange(im, 1, later, g)
            else:
                rows = pl.ds(g * PART, PART)
                for side in range(2):
                    result[0, rows, side * 256 : (side + 1) * 256] = re[side].astype(jnp.bfloat16)
                    result[1, rows, side * 256 : (side + 1) * 256] = im[side].astype(jnp.bfloat16)
                pltpu.make_async_copy(result.at[:, rows], out.at[:, rows], out_sem.at[g]).start()
        now, later = later, now

    for step in range(STEPS):
        finish(step)
    for g in range(CHUNKS):
        rows = pl.ds(g * PART, PART)
        pltpu.make_async_copy(result.at[:, rows], out.at[:, rows], out_sem.at[g]).wait()


def home(stem_tensor, branches, contraction_order, cut_values):
    return pl.pallas_call(
        kernel,
        out_shape=jax.ShapeDtypeStruct(stem_tensor.shape, jnp.bfloat16),
        in_specs=[pl.BlockSpec(memory_space=pltpu.HBM)] * 4,
        out_specs=pl.BlockSpec(memory_space=pltpu.HBM),
        scratch_shapes=[
            pltpu.SMEM(contraction_order.shape, jnp.int32),
            pltpu.SMEM(cut_values.shape, jnp.int32),
            pltpu.VMEM(branches.shape, jnp.bfloat16),
            pltpu.VMEM((2, 1024, 512), jnp.bfloat16),
            pltpu.VMEM((2, 4096, 128), jnp.float32),
            pltpu.VMEM((CHUNKS, PART, 1024), jnp.bfloat16),
            pltpu.VMEM((CHUNKS, PART, 1024), jnp.bfloat16),
            pltpu.VMEM((STEPS, 2, 8, 2, 64, 256), jnp.bfloat16),
            pltpu.VMEM((2, 8, 64, 256), jnp.bfloat16),
            pltpu.VMEM((2, 1024, 512), jnp.bfloat16),
            pltpu.SemaphoreType.DMA((4,)),
            pltpu.SemaphoreType.DMA((CHUNKS,)),
            pltpu.SemaphoreType.DMA((STEPS, 8 + 9)),
            pltpu.SemaphoreType.DMA((STEPS, 8 + 9)),
        ],
        compiler_params=pltpu.CompilerParams(
            collective_id=0, has_side_effects=True, vmem_limit_bytes=62 * 1024 * 1024
        ),
        name="absorb",
    )(contraction_order, cut_values, stem_tensor, branches)


def solution(mesh):
    placed = (
        P(None, ("cuts", "leg", "sub"), None),
        P(None, None, None, "leg", "sub"),
        P(),
        P("cuts"),
    )
    groups = mesh.shape["leg"] * mesh.shape["sub"]

    def body(stem_tensor, *rest):
        square = mesh.shape["leg"] == 8 and mesh.shape["sub"] == 2
        if square and stays_home(groups, stem_tensor.shape[1], stem_tensor.shape[2]):
            return home(stem_tensor, *rest)
        return shards(stem_tensor, *rest)

    return jax.shard_map(
        body,
        mesh=mesh,
        in_specs=placed,
        out_specs=P(None, ("cuts", "leg", "sub"), None),
        check_vma=False,
    )
```
